128 devices in a mesh: aux: 16 (over x, y), orb: 8 (over z, core).
Axes of the slice: x: 4, y: 4, z: 4, core: 2. Of those that a mesh axis runs over, the one named last changes fastest.
Arguments:
- tensor: bfloat16 [24, 1024, 32, 256], P('orb', 'aux'), may hold values from -0.41992188 to 0.41992188
- mu_block: int32 [24, 8], P('orb'), may hold values from 0 to 23, as said below
- green_occ: bfloat16 [768, 768], replicated, may hold values from -0.21875 to 0.21875
- green_virt: bfloat16 [768, 768], replicated, may hold values from -0.21875 to 0.21875
Outputs:
- polarizability: float32 [1024, 1024], P('aux', 'orb')
The draws below stay inside these ranges and needn't reach their ends.
Inputs may be any that keep to these rules, and one draw needn't show every extreme that they name: `mu_block`: row n holds 8 different molecule blocks.
All inputs are finite; a program needn't handle non-finite values.
Results may differ from the reference program's by a relative error of at most 0.0041.
Values may be sent and summed in bfloat16 or wider, within the bound.
No kernel may reach another device: no remote copies, remote signals or barrier semaphores. Data moves between devices by JAX's collectives and lax.ppermute only.
A program may use at most 192 MiB of HBM per device.

```python
import jax
import jax.numpy as jnp
from jax import lax

OB = 32
PER = 8
AUX_DEV = 64
NOB = 24
NO = 768
NAUX = 1024
N_AUX = 16


def draw_mu_block(key, part):
    key = jax.random.fold_in(key, 11)
    row_keys = jax.random.split(key, NOB)
    picked = jax.vmap(lambda row_key: jax.random.permutation(row_key, NOB)[:PER])(row_keys)
    return picked.astype(jnp.int32)


def level_of(stream_key, dims, shards, smallest, largest):
    def one(axis_at, blocks):
        steps = jax.random.uniform(jax.random.fold_in(jax.random.fold_in(stream_key, 6), axis_at), (blocks,), jnp.float32, smallest / len(shards), largest / len(shards))
        return jnp.repeat(jnp.exp(steps), dims[axis_at] // blocks).reshape((-1,) + (1,) * (len(dims) - axis_at - 1))

    factor_of = one(*shards[0])
    for cut in shards[1:]:
        factor_of = factor_of * one(*cut)
    return factor_of


def scatter_about(own_key, shape, deviation, reach, pieces=(), held_as=jnp.bfloat16):
    factor_of = level_of(own_key, shape, pieces, -0.22, 0.18) if pieces else 1.0
    array = jax.random.normal(own_key, shape, jnp.float32) * deviation * factor_of
    return jnp.minimum(jnp.maximum(array, -reach), reach).astype(held_as)


def setup_inputs(seed: int = 0) -> dict:
    seeds = jax.random.split(jax.random.key(seed), 5)
    tensor = scatter_about(seeds[0], (NOB, NAUX, OB, PER * OB), 0.07, 0.41992188, ((0, 8), (1, 16)))
    mu_block = draw_mu_block(jax.random.fold_in(seeds[4], 71), 0)
    green_occ = scatter_about(seeds[2], (NO, NO), NO ** -0.5, 0.21875)
    green_virt = scatter_about(seeds[3], (NO, NO), NO ** -0.5, 0.21875)
    return {"tensor": tensor, "mu_block": mu_block, "green_occ": green_occ, "green_virt": green_virt}


def reference(tensor, mu_block, green_occ, green_virt):
    orbitals = green_occ.shape[0]
    occ_rows = green_occ.reshape(NOB, OB, orbitals)[mu_block].reshape(NOB, PER * OB, orbitals).astype(jnp.float32)
    virt_cols = green_virt.reshape(orbitals, NOB, OB)[:, mu_block].reshape(orbitals, NOB, PER * OB).astype(jnp.float32)

    def one_group(aux_group):
        blocks = aux_group.astype(jnp.float32)
        partial_value = jnp.einsum('npjc,ncl->plnj', blocks, occ_rows).astype(jnp.bfloat16)
        grouped = partial_value.astype(jnp.float32).reshape(AUX_DEV, NOB, OB, orbitals)
        paired = jnp.einsum('pnjv,vnc->pnjc', grouped, virt_cols)
        return paired.astype(jnp.bfloat16)

    groups = tensor.reshape(NOB, N_AUX, AUX_DEV, OB, PER * OB).transpose(1, 0, 2, 3, 4)
    paired = lax.map(one_group, groups).reshape(NAUX, NOB, OB, PER * OB)
    return lax.dot_general(paired.astype(jnp.float32), tensor.astype(jnp.float32), (((1, 2, 3), (0, 2, 3)), ((), ())))
```

```python
import functools

import jax
import jax.numpy as jnp
from jax import lax
from jax.experimental import pallas as pl
from jax.experimental.pallas import tpu as pltpu
from jax.sharding import Mesh
from jax.sharding import PartitionSpec as P

NX, NY, NZ, NC = 4, 4, 4, 2
NXY = NX * NY
BF, F32 = jnp.bfloat16, jnp.float32
LIMIT = 56 * 1024 * 1024


def swap_matrix(outer, inner):
    n = outer * inner
    row = lax.broadcasted_iota(jnp.int32, (n, n), 0)
    col = lax.broadcasted_iota(jnp.int32, (n, n), 1)
    source = (row % outer) * inner + row // outer
    return jnp.where(col == source, 1.0, 0.0).astype(BF)


def regroup_kernel(tensor_ref, swap_ref, out_ref):
    rows = tensor_ref[0].reshape(-1, tensor_ref.shape[-1])
    got = jnp.dot(swap_ref[...], rows, preferred_element_type=F32).astype(BF)
    out_ref[...] = got.reshape(out_ref.shape)


def regroup(tensor, swap):
    blocks, aux, width, pair = tensor.shape
    return pl.pallas_call(
        regroup_kernel,
        grid=(blocks, aux // 16),
        in_specs=[
            pl.BlockSpec((1, 16, width, pair), lambda m, g: (m, g, 0, 0)),
            pl.BlockSpec(swap.shape, lambda m, g: (0, 0)),
        ],
        out_specs=pl.BlockSpec((NXY, 1, 2, 16, pair), lambda m, g: (0, m, 0, g, 0)),
        out_shape=jax.ShapeDtypeStruct((NXY, blocks, 2, aux, pair), BF),
        compiler_params=pltpu.CompilerParams(vmem_limit_bytes=LIMIT),
    )(tensor, swap)


def pair_kernel(mu_nu, mu_lam, *refs):
    pieces = refs[:8]
    occ_ref, virt_ref, swap_ref, out_ref, turned, stage = refs[8:]
    per = mu_nu.shape[1]
    half = occ_ref.shape[1]
    width, pair = 32, 256
    for g in range(6):
        for q in range(4):
            t = g * 4 + q
            piece, m = divmod(t, 3)
            rows = pieces[piece][m].reshape(16 * width, pair)
            occ = jnp.concatenate(
                [
                    occ_ref[pl.ds(pl.multiple_of(mu_nu[t, k] * width, width), width), :]
                    for k in range(per)
                ],
                axis=0,
            )
            got = jnp.dot(rows, occ, preferred_element_type=F32).astype(BF)
            stage[:, q * width : (q + 1) * width, :] = got.reshape(16, width, half)
        for p in range(16):
            turned[p, :, g * 128 : (g + 1) * 128] = stage[p].T

    @pl.loop(0, 4)
    def _(z):
        for m in range(3):
            lam = z * 3 + m
            left = turned[:, pl.ds(pl.multiple_of(lam * width, width), width), :]
            left = left.reshape(16 * width, -1)
            virt = jnp.concatenate(
                [
                    virt_ref[pl.ds(pl.multiple_of(mu_lam[lam, k] * width, width), width), :]
                    for k in range(per)
                ],
                axis=0,
            )
            got = lax.dot_general(
                left, virt, (((1,), (1,)), ((), ())), preferred_element_type=F32
            ).astype(BF)
            got = jnp.dot(swap_ref[...], got, preferred_element_type=F32).astype(BF)
            out_ref[:, z, m, :, :] = got.reshape(16, 32, pair)


def make_paired(mu_nu, mu_lam, pieces, occ, virt, swap):
    orbitals, half = occ.shape
    vmem = pl.BlockSpec(memory_space=pltpu.VMEM)
    smem = pl.BlockSpec(memory_space=pltpu.SMEM)
    return pl.pallas_call(
        pair_kernel,
        in_specs=[smem, smem] + [vmem] * 11,
        out_specs=vmem,
        out_shape=jax.ShapeDtypeStruct((NXY, NZ, 3, 32, 256), BF),
        scratch_shapes=[
            pltpu.VMEM((16, half, orbitals), BF),
            pltpu.VMEM((16, 128, half), BF),
        ],
        compiler_params=pltpu.CompilerParams(vmem_limit_bytes=LIMIT),
    )(mu_nu, mu_lam, *pieces, occ, virt, swap)


def chi_kernel(core, a_ref, b_ref, out_ref):
    @pl.when(pl.program_id(0) == 0)
    def _():
        out_ref[...] = jnp.zeros_like(out_ref)

    for r in range(2):
        a = a_ref[:, 0, r * 16 : (r + 1) * 16, :].reshape(-1, a_ref.shape[-1])
        for z in range(4):
            b = b_ref[z, 0, :, 0, r].reshape(-1, b_ref.shape[-1])
            out_ref[:, z, :] += lax.dot_general(
                a, b, (((1,), (1,)), ((), ())), preferred_element_type=F32
            )


def chi_half(core, a, b):
    return pl.pallas_call(
        chi_kernel,
        grid_spec=pltpu.PrefetchScalarGridSpec(
            num_scalar_prefetch=1,
            grid=(3,),
            in_specs=[
                pl.BlockSpec((64, 1, 32, 256), lambda m, core: (0, m, 0, 0)),
                pl.BlockSpec(
                    (4, 1, 2, 1, 2, 64, 256), lambda m, core: (0, core[0], 0, m, 0, 0, 0)
                ),
            ],
            out_specs=pl.BlockSpec((1024, 4, 128), lambda m, core: (0, 0, 0)),
        ),
        out_shape=jax.ShapeDtypeStruct((1024, 4, 128), F32),
        compiler_params=pltpu.CompilerParams(vmem_limit_bytes=LIMIT),
    )(core, a, b)


def shards(tensor, mu_block, green_occ, green_virt):
    z, core = lax.axis_index("z"), lax.axis_index("core")
    orbitals = green_occ.shape[0]
    other = [(0, 1), (1, 0)]
    swap = swap_matrix(16, 32)

    by_z = tensor.reshape(3, NZ, 16, 32, 256)
    arrived = []
    for s in range(NZ):
        block = lax.dynamic_index_in_dim(by_z, (z + s) % NZ, 1, keepdims=False)
        if s:
            block = lax.ppermute(block, "z", [(i, (i + s) % NZ) for i in range(NZ)])
        arrived.append(block)
    pieces = []
    for block in arrived:
        pieces += [block, lax.ppermute(block, "core", other)]

    q_side = lax.all_to_all(
        regroup(tensor, swap), ("x", "y"), split_axis=0, concat_axis=0, tiled=True
    )

    mu_all = lax.all_gather(mu_block, ("z", "core"), axis=0, tiled=True)
    order = jnp.stack(
        [((z - s) % NZ) * NC + c for s in range(NZ) for c in (core, 1 - core)]
    )
    mu_nu = mu_all.reshape(NZ * NC, 3, -1)[order].reshape(NZ * NC * 3, -1)
    mu_lam = lax.dynamic_index_in_dim(
        mu_all.reshape(NZ, NC, 3, -1), core, 1, keepdims=False
    ).reshape(NZ * 3, -1)
    occ = lax.dynamic_index_in_dim(
        green_occ.reshape(orbitals, NZ, NC, -1), core, 2, keepdims=False
    ).reshape(orbitals, -1)
    virt = green_virt.reshape(NZ * NC, -1, orbitals)[order].reshape(orbitals, orbitals).T

    paired = make_paired(mu_nu, mu_lam, pieces, occ, virt, swap)
    p_side = lax.all_to_all(
        paired.reshape(NXY * NZ, 3, 32, 256), ("x", "y", "z"), 0, 0, tiled=True
    )
    q_side = q_side.reshape(4, 2, 2, 3, 2, 64, 256)
    given = chi_half((1 - core).reshape(1), p_side, q_side)
    kept = chi_half(core.reshape(1), p_side, q_side)
    chi = kept + lax.ppermute(given, "core", other)

    chi = chi.reshape(NXY, 64, NZ, 128).transpose(0, 2, 1, 3).reshape(NXY * NZ, 64, 128)
    shares = lax.all_to_all(chi, ("x", "y", "z"), 0, 0, tiled=True)
    return shares.reshape(NXY * NZ, 64, 128).sum(0)


def solution(mesh):
    mesh = Mesh(mesh.devices.reshape(NX, NY, NZ, NC), ("x", "y", "z", "core"))
    return jax.shard_map(
        shards,
        mesh=mesh,
        in_specs=(P(("z", "core"), ("x", "y"), None, None), P(("z", "core"), None), P(), P()),
        out_specs=P(("x", "y"), ("z", "core")),
        check_vma=False,
    )
```

```python
import jax
import jax.numpy as jnp
from jax import lax
from jax.experimental import pallas as pl
from jax.experimental.pallas import tpu as pltpu
from jax.sharding import Mesh
from jax.sharding import PartitionSpec as P

NX, NY, NZ, NC = 4, 4, 4, 2
NXY = NX * NY
BF, F32 = jnp.bfloat16, jnp.float32
LIMIT = 56 * 1024 * 1024


def regroup_kernel(tensor_ref, out_ref):
    out_ref[:, 0] = jnp.swapaxes(tensor_ref[0], 0, 1).reshape(
        NXY, 2, tensor_ref.shape[1], tensor_ref.shape[3]
    )


def regroup(tensor):
    blocks, aux, width, pair = tensor.shape
    return pl.pallas_call(
        regroup_kernel,
        grid=(blocks,),
        in_specs=[pl.BlockSpec((1, aux, width, pair), lambda m: (m, 0, 0, 0))],
        out_specs=pl.BlockSpec((NXY, 1, 2, aux, pair), lambda m: (0, m, 0, 0, 0)),
        out_shape=jax.ShapeDtypeStruct((NXY, blocks, 2, aux, pair), BF),
        compiler_params=pltpu.CompilerParams(vmem_limit_bytes=LIMIT),
        cost_estimate=pl.CostEstimate(
            flops=1000, bytes_accessed=1000, transcendentals=0
        ),
    )(tensor)


def gathered(ref, mu, t, per, width):
    return jnp.concatenate(
        [ref[pl.ds(pl.multiple_of(mu[t, k] * width, width), width), :] for k in range(per)],
        axis=0,
    )


def pair_kernel(z_ref, *refs):
    mus, pieces = refs[:4], refs[4:12]
    occ_ref, virt_ref, out_ref, turned, stage = refs[12:]
    per, half, width, pair = mus[0].shape[1], occ_ref.shape[1], 32, 256
    for g in range(6):
        for q in range(4):
            piece, m = divmod(g * 4 + q, 3)
            rows = pieces[piece][m].reshape(16 * width, pair)
            occ = gathered(occ_ref, mus[piece // 2], piece % 2 * 3 + m, per, width)
            got = jnp.dot(rows, occ, preferred_element_type=F32).astype(BF)
            stage[:, q * width : (q + 1) * width, :] = got.reshape(16, width, half)
        for p in range(16):
            turned[p, :, g * 128 : (g + 1) * 128] = stage[p].T

    for s in range(NZ):
        z = lax.rem(z_ref[0] - s + NZ, NZ)
        for m in range(3):
            lam = pl.multiple_of((z * 3 + m) * width, width)
            left = turned[:, pl.ds(lam, width), :].reshape(16 * width, -1)
            virt = gathered(virt_ref, mus[s], m, per, width)
            got = lax.dot_general(
                left, virt, (((1,), (1,)), ((), ())), preferred_element_type=F32
            ).astype(BF)
            got = jnp.swapaxes(got.reshape(16, width, pair), 0, 1)
            out_ref[:, z, m, :, :] = got.reshape(NXY, 32, pair)


def make_paired(z, mus, pieces, occ, virt):
    orbitals, half = occ.shape
    vmem = pl.BlockSpec(memory_space=pltpu.VMEM)
    smem = pl.BlockSpec(memory_space=pltpu.SMEM)
    return pl.pallas_call(
        pair_kernel,
        in_specs=[smem] * 5 + [vmem] * 10,
        out_specs=vmem,
        out_shape=jax.ShapeDtypeStruct((NXY, NZ, 3, 32, 256), BF),
        scratch_shapes=[
            pltpu.VMEM((16, half, orbitals), BF),
            pltpu.VMEM((16, 128, half), BF),
        ],
        compiler_params=pltpu.CompilerParams(vmem_limit_bytes=LIMIT),
        cost_estimate=pl.CostEstimate(
            flops=22_000_000_000, bytes_accessed=12_000_000, transcendentals=0
        ),
    )(z, *mus, *pieces, occ, virt)


def chi_kernel(core, a_ref, b_ref, out_ref):
    pair = a_ref.shape[-1]
    a = jnp.concatenate(
        [a_ref[:, 0, r * 16 : (r + 1) * 16, :].reshape(-1, pair) for r in range(2)], axis=1
    )
    b = jnp.concatenate([b_ref[:, 0, :, 0, r].reshape(-1, pair) for r in range(2)], axis=1)
    got = lax.dot_general(a, b, (((1,), (1,)), ((), ())), preferred_element_type=F32)
    first = pl.program_id(0) == 0

    @pl.when(first)
    def _():
        for z in range(NZ):
            out_ref[:, z] = got[:, z * 128 : (z + 1) * 128].reshape(NXY, 64, 128)

    @pl.when(jnp.logical_not(first))
    def _():
        for z in range(NZ):
            out_ref[:, z] += got[:, z * 128 : (z + 1) * 128].reshape(NXY, 64, 128)


def chi_half(core, a, b):
    return pl.pallas_call(
        chi_kernel,
        grid_spec=pltpu.PrefetchScalarGridSpec(
            num_scalar_prefetch=1,
            grid=(3,),
            in_specs=[
                pl.BlockSpec((64, 1, 32, 256), lambda m, core: (0, m, 0, 0)),
                pl.BlockSpec(
                    (4, 1, 2, 1, 2, 64, 256), lambda m, core: (0, core[0], 0, m, 0, 0, 0)
                ),
            ],
            out_specs=pl.BlockSpec((NXY, NZ, 64, 128), lambda m, core: (0, 0, 0, 0)),
        ),
        out_shape=jax.ShapeDtypeStruct((NXY, NZ, 64, 128), F32),
        compiler_params=pltpu.CompilerParams(vmem_limit_bytes=LIMIT),
        cost_estimate=pl.CostEstimate(
            flops=1_700_000_000, bytes_accessed=7_000_000, transcendentals=0
        ),
    )(core, a, b)


def shards(tensor, mu_block, green_occ, green_virt):
    z, core = lax.axis_index("z"), lax.axis_index("core")
    orbitals = green_occ.shape[0]
    other = [(0, 1), (1, 0)]
    around = [[(i, (i + s) % NZ) for i in range(NZ)] for s in range(NZ)]

    by_z = tensor.reshape(3, NZ, 16, 32, 256)
    blocks = [
        lax.dynamic_index_in_dim(by_z, (z + s) % NZ, 1, keepdims=False) for s in range(NZ)
    ]
    mu_pair = jnp.concatenate([mu_block, lax.ppermute(mu_block, "core", other)], axis=0)
    mus = [lax.ppermute(mu_pair, "z", around[s]) for s in range(1, NZ)]
    mus, blocks = lax.optimization_barrier((mus, blocks))
    arrived = [lax.ppermute(blocks[s], "z", around[s]) for s in range(1, NZ)]
    own_other = lax.ppermute(blocks[0], "core", other)

    occ = lax.dynamic_index_in_dim(
        green_occ.reshape(orbitals, NZ, NC, -1), core, 2, keepdims=False
    ).reshape(orbitals, -1)
    order = jnp.stack(
        [((z - s) % NZ) * NC + c for s in range(NZ) for c in (core, 1 - core)]
    )
    virt = green_virt.reshape(NZ * NC, -1, orbitals)[order].reshape(orbitals, orbitals).T
    held, own_other, occ, virt = lax.optimization_barrier((tensor, own_other, occ, virt))
    q_side = lax.all_to_all(
        regroup(held), ("x", "y"), split_axis=0, concat_axis=0, tiled=True
    )


    pieces = [blocks[0], own_other]
    for block in arrived:
        pieces += [block, lax.ppermute(block, "core", other)]
    paired = make_paired(z.reshape(1), [mu_pair, *mus], pieces, occ, virt)
    p_side = lax.all_to_all(
        paired.reshape(NXY * NZ, 3, 32, 256), ("x", "y", "z"), 0, 0, tiled=True
    )
    q_side = q_side.reshape(4, 2, 2, 3, 2, 64, 256)
    given = chi_half((1 - core).reshape(1), p_side, q_side)
    kept = chi_half(core.reshape(1), p_side, q_side)
    chi = (kept + lax.ppermute(given, "core", other)).astype(BF)
    shares = lax.all_to_all(
        chi.reshape(NXY * NZ, 64, 128), ("x", "y", "z"), 0, 0, tiled=True
    )
    return shares.astype(F32).sum(0)


def solution(mesh):
    mesh = Mesh(mesh.devices.reshape(NX, NY, NZ, NC), ("x", "y", "z", "core"))
    return jax.shard_map(
        shards,
        mesh=mesh,
        in_specs=(P(("z", "core"), ("x", "y"), None, None), P(("z", "core"), None), P(), P()),
        out_specs=P(("x", "y"), ("z", "core")),
        check_vma=False,
    )
```

```python
import jax
import jax.numpy as jnp
from jax import lax
from jax.experimental import pallas as pl
from jax.experimental.pallas import tpu as pltpu
from jax.sharding import Mesh
from jax.sharding import PartitionSpec as P

NX, NY, NZ, NC = 4, 4, 4, 2
NXY = NX * NY
BF, F32 = jnp.bfloat16, jnp.float32
LIMIT = 30 * 1024 * 1024
PAIR_FLOPS = 22_000_000_000


def spread_kernel(z_ref, tensor_ref, mu_ref, *outs):
    regrouped, blocks = outs[0], outs[1:]
    rows, pair = 16 * tensor_ref.shape[2], tensor_ref.shape[3]
    regrouped[:, 0] = jnp.swapaxes(tensor_ref[0], 0, 1).reshape(
        NXY, 2, tensor_ref.shape[1], pair
    )
    for s in range(NZ):
        z = lax.rem(z_ref[0] + s, NZ)
        blocks[s][0, :rows] = tensor_ref[0, pl.ds(z * 16, 16)].reshape(rows, pair)
        blocks[s][0, rows:] = mu_ref[0]


def spread(z, tensor, mu_rows):
    blocks, aux, width, pair = tensor.shape
    piece = (16 * width + 16, pair)
    return pl.pallas_call(
        spread_kernel,
        grid_spec=pltpu.PrefetchScalarGridSpec(
            num_scalar_prefetch=1,
            grid=(blocks,),
            in_specs=[
                pl.BlockSpec((1, aux, width, pair), lambda m, z: (m, 0, 0, 0)),
                pl.BlockSpec((1, 16, pair), lambda m, z: (m, 0, 0)),
            ],
            out_specs=[pl.BlockSpec((NXY, 1, 2, aux, pair), lambda m, z: (0, m, 0, 0, 0))]
            + [pl.BlockSpec((1, *piece), lambda m, z: (m, 0, 0))] * NZ,
        ),
        out_shape=[pltpu.HBM((NXY, blocks, 2, aux, pair), BF)]
        + [jax.ShapeDtypeStruct((blocks, *piece), BF)] * NZ,
        compiler_params=pltpu.CompilerParams(vmem_limit_bytes=LIMIT),
        cost_estimate=pl.CostEstimate(flops=1000, bytes_accessed=1000, transcendentals=0),
    )(z, tensor, mu_rows)


def gathered(ref, mu, t, per, width):
    return jnp.concatenate(
        [ref[pl.ds(pl.multiple_of(mu[t, k] * width, width), width), :] for k in range(per)],
        axis=0,
    )


def occupied(piece, mu, m, at, occ_ref, stage):
    per, half, width = mu.shape[1], occ_ref.shape[1], 32
    occ = gathered(occ_ref, mu, at[0], per, width)
    got = jnp.dot(piece[m, : 16 * width], occ, preferred_element_type=F32).astype(BF)
    stage[:, at[1] : at[1] + width, :] = got.reshape(16, width, half)


def early_kernel(mu_own, mu_other, own, other, occ_ref, out_ref, stage):
    stage[:, :64, :] = jnp.zeros((16, 64, stage.shape[2]), BF)
    for n in range(6):
        piece, mu = ((own, mu_own), (other, mu_other))[n // 3]
        occupied(piece, mu, n % 3, (n % 3, 64 + n * 32), occ_ref, stage)
    for p in range(16):
        for g in range(2):
            out_ref[p, :, g * 128 : (g + 1) * 128] = stage[p, g * 128 : (g + 1) * 128].T


def make_early(mu_own, mu_other, own, other, occ):
    half = occ.shape[1]
    vmem = pl.BlockSpec(memory_space=pltpu.VMEM)
    smem = pl.BlockSpec(memory_space=pltpu.SMEM)
    return pl.pallas_call(
        early_kernel,
        in_specs=[smem] * 2 + [vmem] * 3,
        out_specs=vmem,
        out_shape=jax.ShapeDtypeStruct((16, half, 256), BF),
        scratch_shapes=[pltpu.VMEM((16, 256, half), BF)],
        compiler_params=pltpu.CompilerParams(vmem_limit_bytes=LIMIT),
        cost_estimate=pl.CostEstimate(flops=1000, bytes_accessed=1000, transcendentals=0),
    )(mu_own, mu_other, own, other, occ)


def pair_kernel(z_ref, mu_own, mu_other, *refs):
    pieces, refs = refs[:6], refs[6:]
    occ_ref, virt_ref, early_ref, out_ref, turned, stage, result, out_sems = refs
    per, width, pair = mu_own.shape[1], 32, 256
    for n in range(18):
        piece, m = divmod(n, 3)
        mu = mu_other if piece % 2 else mu_own
        at = ((piece // 2 + 1) * 3 + m, n % 4 * width)
        occupied(pieces[piece], mu, m, at, occ_ref, stage)
        if n % 4 == 3:
            for p in range(16):
                turned[p, :, (n - 3) * width : (n + 1) * width] = stage[p].T
    turned[:, :, 512:] = early_ref[...]
    for p in range(16):
        turned[p, :, 512:576] = stage[p, :64].T
    stores = []
    for z in range(NZ):
        s = lax.rem(z_ref[0] - z + NZ, NZ)
        for m in range(3):
            lam = (z * 3 + m) * width
            left = turned[:, lam : lam + width, :].reshape(16 * width, -1)
            virt = gathered(virt_ref, mu_own, s * 3 + m, per, width)
            got = lax.dot_general(
                left, virt, (((1,), (1,)), ((), ())), preferred_element_type=F32
            ).astype(BF)
            got = jnp.swapaxes(got.reshape(16, width, pair), 0, 1)
            result[z, :, m, :, :] = got.reshape(NXY, 32, pair)
        stores.append(
            pltpu.make_async_copy(result.at[z], out_ref.at[:, z], out_sems.at[z])
        )
        stores[z].start()
    for store in stores:
        store.wait()


def make_paired(z, mu_own, mu_other, pieces, occ, virt, early):
    orbitals, half = occ.shape
    smem = pl.BlockSpec(memory_space=pltpu.SMEM)
    return pl.pallas_call(
        pair_kernel,
        in_specs=[smem] * 3 + [pl.BlockSpec(memory_space=pltpu.VMEM)] * 9,
        out_specs=pl.BlockSpec(memory_space=pltpu.HBM),
        out_shape=pltpu.HBM((NXY, NZ, 3, 32, 256), BF),
        scratch_shapes=[
            pltpu.VMEM((16, half, orbitals), BF),
            pltpu.VMEM((16, 128, half), BF),
            pltpu.VMEM((NZ, NXY, 3, 32, 256), BF),
            pltpu.SemaphoreType.DMA((NZ,)),
        ],
        compiler_params=pltpu.CompilerParams(vmem_limit_bytes=LIMIT),
        cost_estimate=pl.CostEstimate(
            flops=PAIR_FLOPS, bytes_accessed=12_000_000, transcendentals=0
        ),
    )(z, mu_own, mu_other, *pieces, occ, virt, early)


def listed_kernel(mu_ref, *refs):
    per = mu_ref.shape[1]
    refs[-1][:3] = mu_ref[...]
    for s in range(1, NZ):
        refs[-1][s * 3 : s * 3 + 3] = refs[s - 1][:, 0, :per].astype(F32).astype(jnp.int32)


def listed(mu_block, pieces):
    blocks, per = mu_block.shape
    tile = pl.BlockSpec((blocks, 16, 256), lambda i: (0, 32, 0))
    return pl.pallas_call(
        listed_kernel,
        grid=(1,),
        in_specs=[pl.BlockSpec((blocks, per), lambda i: (0, 0))] + [tile] * 3,
        out_specs=pl.BlockSpec((NZ * blocks, per), lambda i: (0, 0)),
        out_shape=jax.ShapeDtypeStruct((NZ * blocks, per), jnp.int32),
        compiler_params=pltpu.CompilerParams(vmem_limit_bytes=LIMIT),
    )(mu_block, *pieces)


def chi_kernel(core, a_ref, b_ref, out_ref):
    pair, parts = a_ref.shape[-1], [(m, r) for m in range(3) for r in range(2)]
    a = jnp.concatenate(
        [a_ref[:, m, r * 16 : (r + 1) * 16, :].reshape(-1, pair) for m, r in parts], axis=1
    )
    b = jnp.concatenate([b_ref[:, 0, :, m, r].reshape(-1, pair) for m, r in parts], axis=1)
    got = lax.dot_general(a, b, (((1,), (1,)), ((), ())), preferred_element_type=F32)
    for z in range(NZ):
        out_ref[:, z] = got[:, z * 128 : (z + 1) * 128].reshape(-1, 64, 128)


def chi_half(core, a, b):
    return pl.pallas_call(
        chi_kernel,
        grid_spec=pltpu.PrefetchScalarGridSpec(
            num_scalar_prefetch=1,
            grid=(2,),
            in_specs=[
                pl.BlockSpec((32, 3, 32, 256), lambda i, core: (i, 0, 0, 0)),
                pl.BlockSpec(
                    (4, 1, 2, 3, 2, 64, 256), lambda i, core: (0, core[0], 0, 0, 0, 0, 0)
                ),
            ],
            out_specs=pl.BlockSpec((8, NZ, 64, 128), lambda i, core: (i, 0, 0, 0)),
        ),
        out_shape=jax.ShapeDtypeStruct((NXY, NZ, 64, 128), F32),
        compiler_params=pltpu.CompilerParams(vmem_limit_bytes=LIMIT),
        cost_estimate=pl.CostEstimate(
            flops=1_700_000_000, bytes_accessed=7_000_000, transcendentals=0
        ),
    )(core, a, b)


def shards(tensor, mu_block, green_occ, green_virt):
    z, core = lax.axis_index("z"), lax.axis_index("core")
    orbitals = green_occ.shape[0]
    other = [(0, 1), (1, 0)]
    around = [[(i, (i + s) % NZ) for i in range(NZ)] for s in range(NZ)]

    mu_rows = jnp.pad(mu_block[:, None, :], ((0, 0), (0, 15), (0, 256 - mu_block.shape[1])))
    regrouped, *blocks = spread(z.reshape(1), tensor, mu_rows.astype(BF))
    arrived = [lax.ppermute(blocks[s], "z", around[s]) if s else blocks[0] for s in range(NZ)]
    q_side = lax.all_to_all(regrouped, ("x", "y"), split_axis=0, concat_axis=0, tiled=True)

    occ = lax.dynamic_index_in_dim(
        green_occ.reshape(orbitals, NZ, NC, -1), core, 2, keepdims=False
    ).reshape(orbitals, -1)
    order = jnp.stack(
        [((z - s) % NZ) * NC + c for s in (1, 2, 3, 0) for c in (core, 1 - core)]
    )
    virt = green_virt.reshape(NZ * NC, -1, orbitals)[order].reshape(orbitals, orbitals).T

    early = make_early(
        mu_block,
        lax.ppermute(mu_block, "core", other),
        blocks[0],
        lax.ppermute(blocks[0], "core", other),
        occ,
    )
    early, virt, *tail = lax.optimization_barrier((early, virt, *arrived[2:]))
    arrived = [arrived[1], *tail]
    mu_own = listed(mu_block, arrived)
    pieces = [q for p in arrived for q in (p, lax.ppermute(p, "core", other))]
    paired = make_paired(
        z.reshape(1), mu_own, lax.ppermute(mu_own, "core", other), pieces, occ, virt, early
    )
    p_side = lax.all_to_all(
        paired.reshape(NXY * NZ, 3, 32, 256), ("x", "y", "z"), 0, 0, tiled=True
    )
    q_side = q_side.reshape(4, 2, 2, 3, 2, 64, 256)
    given = chi_half((1 - core).reshape(1), p_side, q_side)
    kept = chi_half(core.reshape(1), p_side, q_side)
    chi = (kept + lax.ppermute(given, "core", other)).astype(BF)
    shares = lax.all_to_all(
        chi.reshape(NXY * NZ, 64, 128), ("x", "y", "z"), 0, 0, tiled=True
    )
    return shares.astype(F32).sum(0)


def solution(mesh):
    mesh = Mesh(mesh.devices.reshape(NX, NY, NZ, NC), ("x", "y", "z", "core"))
    return jax.shard_map(
        shards,
        mesh=mesh,
        in_specs=(P(("z", "core"), ("x", "y"), None, None), P(("z", "core"), None), P(), P()),
        out_specs=P(("x", "y"), ("z", "core")),
        check_vma=False,
    )
```

```python
import jax
import jax.numpy as jnp
from jax import lax
from jax.experimental import pallas as pl
from jax.experimental.pallas import tpu as pltpu
from jax.sharding import Mesh
from jax.sharding import PartitionSpec as P

NX, NY, NZ, NC = 4, 4, 4, 2
NXY = NX * NY
BF, F32 = jnp.bfloat16, jnp.float32
LIMIT = 30 * 1024 * 1024
PAIR_FLOPS = 15_000_000_000


def spread_kernel(z_ref, mu_ref, tensor_ref, *refs):
    regrouped, blocks = refs[0], refs[1 : 1 + NZ]
    held, turned, listed, in_sems, out_sems, cut_sems, mu_sems = refs[1 + NZ :]
    count, aux, width, pair = tensor_ref.shape
    loads = [
        pltpu.make_async_copy(tensor_ref.at[m], held.at[m], in_sems.at[m])
        for m in range(count)
    ]
    for load in loads:
        load.start()
    lane = lax.broadcasted_iota(jnp.int32, (width, pair), 1)
    for m in range(count):
        tile = jnp.zeros((width, pair), jnp.int32)
        for k in range(mu_ref.shape[1]):
            tile = jnp.where(lane == k, mu_ref[m, k], tile)
        listed[m, 0] = tile.astype(F32).astype(BF)
    copies = []
    for s in range(NZ):
        to = blocks[s].at[:, pl.ds(16, 1)]
        copies.append(pltpu.make_async_copy(listed, to, mu_sems.at[s]))
        copies[-1].start()
    for m in range(count):
        loads[m].wait()
        for s in range(NZ):
            z = lax.rem(z_ref[0] + s, NZ)
            copies.append(
                pltpu.make_async_copy(
                    held.at[m, pl.ds(z * 16, 16)],
                    blocks[s].at[m, pl.ds(0, 16)],
                    cut_sems.at[m * NZ + s],
                )
            )
            copies[-1].start()
        turned[m] = jnp.swapaxes(held[m], 0, 1).reshape(NXY, 2, aux, pair)
        copies.append(
            pltpu.make_async_copy(turned.at[m], regrouped.at[:, m], out_sems.at[m])
        )
        copies[-1].start()
    for copy in copies:
        copy.wait()


def spread(z, mu, tensor):
    blocks, aux, width, pair = tensor.shape
    smem = pl.BlockSpec(memory_space=pltpu.SMEM)
    anywhere = pl.BlockSpec(memory_space=pl.ANY)
    return pl.pallas_call(
        spread_kernel,
        in_specs=[smem, smem, anywhere],
        out_specs=[anywhere] * (1 + NZ),
        out_shape=[pltpu.HBM((NXY, blocks, 2, aux, pair), BF)]
        + [jax.ShapeDtypeStruct((blocks, 17, width, pair), BF)] * NZ,
        scratch_shapes=[
            pltpu.VMEM(tensor.shape, BF),
            pltpu.VMEM((blocks, NXY, 2, aux, pair), BF),
            pltpu.VMEM((blocks, 1, width, pair), BF),
            pltpu.SemaphoreType.DMA((blocks,)),
            pltpu.SemaphoreType.DMA((blocks,)),
            pltpu.SemaphoreType.DMA((blocks * NZ,)),
            pltpu.SemaphoreType.DMA((NZ,)),
        ],
        compiler_params=pltpu.CompilerParams(vmem_limit_bytes=60 * 1024 * 1024),
        cost_estimate=pl.CostEstimate(flops=1000, bytes_accessed=1000, transcendentals=0),
    )(z, mu, tensor)


def gathered(ref, mu, t, per, width):
    return jnp.concatenate(
        [ref[pl.ds(pl.multiple_of(mu[t, k] * width, width), width), :] for k in range(per)],
        axis=0,
    )


def occupied(piece, mu, m, at, occ_ref, stage):
    per, half, width = mu.shape[1], occ_ref.shape[1], 32
    occ = gathered(occ_ref, mu, at[0], per, width)
    got = jnp.dot(
        piece[m, :16].reshape(16 * width, -1), occ, preferred_element_type=F32
    ).astype(BF)
    stage[:, at[1] : at[1] + width, :] = got.reshape(16, width, half)


def early_kernel(mu_own, mu_other, own, other, occ_ref, out_ref, stage):
    stage[:, :64, :] = jnp.zeros((16, 64, stage.shape[2]), BF)
    for n in range(6):
        piece, mu = ((own, mu_own), (other, mu_other))[n // 3]
        occupied(piece, mu, n % 3, (n % 3, 64 + n * 32), occ_ref, stage)
    for p in range(16):
        for g in range(2):
            out_ref[p, :, g * 128 : (g + 1) * 128] = stage[p, g * 128 : (g + 1) * 128].T


def make_early(mu_own, mu_other, own, other, occ):
    half = occ.shape[1]
    vmem = pl.BlockSpec(memory_space=pltpu.VMEM)
    smem = pl.BlockSpec(memory_space=pltpu.SMEM)
    return pl.pallas_call(
        early_kernel,
        in_specs=[smem] * 2 + [vmem] * 3,
        out_specs=vmem,
        out_shape=jax.ShapeDtypeStruct((16, half, 256), BF),
        scratch_shapes=[pltpu.VMEM((16, 256, half), BF)],
        compiler_params=pltpu.CompilerParams(vmem_limit_bytes=LIMIT),
        cost_estimate=pl.CostEstimate(flops=1000, bytes_accessed=1000, transcendentals=0),
    )(mu_own, mu_other, own, other, occ)


def pair_kernel(z_ref, mu_own, mu_other, *refs):
    pieces, refs = refs[:6], refs[6:]
    occ_ref, virt_ref, early_ref, out_ref, turned, stage, result, out_sems = refs
    per, width, pair = mu_own.shape[1], 32, 256
    for n in range(18):
        piece, m = divmod(n, 3)
        mu = mu_other if piece % 2 else mu_own
        at = ((piece // 2 + 1) * 3 + m, n % 4 * width)
        occupied(pieces[piece], mu, m, at, occ_ref, stage)
        if n % 4 == 3:
            for p in range(16):
                turned[p, :, (n - 3) * width : (n + 1) * width] = stage[p].T
    turned[:, :, 512:] = early_ref[...]
    for p in range(16):
        turned[p, :, 512:576] = stage[p, :64].T
    stores = []
    for z in range(NZ):
        s = lax.rem(z_ref[0] - z + NZ, NZ)
        for m in range(3):
            lam = (z * 3 + m) * width
            left = turned[:, lam : lam + width, :].reshape(16 * width, -1)
            virt = gathered(virt_ref, mu_own, s * 3 + m, per, width)
            got = lax.dot_general(
                left, virt, (((1,), (1,)), ((), ())), preferred_element_type=F32
            ).astype(BF)
            got = jnp.swapaxes(got.reshape(16, width, pair), 0, 1)
            result[z, :, m, :, :] = got.reshape(NXY, 32, pair)
        stores.append(
            pltpu.make_async_copy(result.at[z], out_ref.at[:, z], out_sems.at[z])
        )
        stores[z].start()
    for store in stores:
        store.wait()


def make_paired(z, mu_own, mu_other, pieces, occ, virt, early):
    orbitals, half = occ.shape
    smem = pl.BlockSpec(memory_space=pltpu.SMEM)
    return pl.pallas_call(
        pair_kernel,
        in_specs=[smem] * 3 + [pl.BlockSpec(memory_space=pltpu.VMEM)] * 9,
        out_specs=pl.BlockSpec(memory_space=pltpu.HBM),
        out_shape=pltpu.HBM((NXY, NZ, 3, 32, 256), BF),
        scratch_shapes=[
            pltpu.VMEM((16, half, orbitals), BF),
            pltpu.VMEM((16, 128, half), BF),
            pltpu.VMEM((NZ, NXY, 3, 32, 256), BF),
            pltpu.SemaphoreType.DMA((NZ,)),
        ],
        compiler_params=pltpu.CompilerParams(vmem_limit_bytes=LIMIT),
        cost_estimate=pl.CostEstimate(
            flops=PAIR_FLOPS, bytes_accessed=12_000_000, transcendentals=0
        ),
    )(z, mu_own, mu_other, *pieces, occ, virt, early)


def listed_kernel(mu_ref, *refs):
    per = mu_ref.shape[1]
    refs[-1][:3] = mu_ref[...]
    for s in range(1, NZ):
        refs[-1][s * 3 : s * 3 + 3] = refs[s - 1][:, 0, 0, :per].astype(F32).astype(jnp.int32)


def listed(mu_block, pieces):
    blocks, per = mu_block.shape
    tile = pl.BlockSpec((blocks, 1, 32, 256), lambda i: (0, 16, 0, 0))
    return pl.pallas_call(
        listed_kernel,
        grid=(1,),
        in_specs=[pl.BlockSpec((blocks, per), lambda i: (0, 0))] + [tile] * 3,
        out_specs=pl.BlockSpec((NZ * blocks, per), lambda i: (0, 0)),
        out_shape=jax.ShapeDtypeStruct((NZ * blocks, per), jnp.int32),
        compiler_params=pltpu.CompilerParams(vmem_limit_bytes=LIMIT),
    )(mu_block, *pieces)


def chi_kernel(core, a_ref, b_ref, out_ref):
    pair, parts = a_ref.shape[-1], [(m, r) for m in range(3) for r in range(2)]
    a = jnp.concatenate(
        [a_ref[:, m, r * 16 : (r + 1) * 16, :].reshape(-1, pair) for m, r in parts], axis=1
    )
    b = jnp.concatenate([b_ref[:, 0, :, m, r].reshape(-1, pair) for m, r in parts], axis=1)
    got = lax.dot_general(a, b, (((1,), (1,)), ((), ())), preferred_element_type=F32)
    for z in range(NZ):
        out_ref[:, z] = got[:, z * 128 : (z + 1) * 128].reshape(-1, 64, 128)


def chi_half(core, a, b):
    return pl.pallas_call(
        chi_kernel,
        grid_spec=pltpu.PrefetchScalarGridSpec(
            num_scalar_prefetch=1,
            grid=(2,),
            in_specs=[
                pl.BlockSpec((32, 3, 32, 256), lambda i, core: (i, 0, 0, 0)),
                pl.BlockSpec(
                    (4, 1, 2, 3, 2, 64, 256), lambda i, core: (0, core[0], 0, 0, 0, 0, 0)
                ),
            ],
            out_specs=pl.BlockSpec((8, NZ, 64, 128), lambda i, core: (i, 0, 0, 0)),
        ),
        out_shape=jax.ShapeDtypeStruct((NXY, NZ, 64, 128), F32),
        compiler_params=pltpu.CompilerParams(vmem_limit_bytes=LIMIT),
        cost_estimate=pl.CostEstimate(
            flops=1_700_000_000, bytes_accessed=7_000_000, transcendentals=0
        ),
    )(core, a, b)


def shards(tensor, mu_block, green_occ, green_virt):
    z, core = lax.axis_index("z"), lax.axis_index("core")
    orbitals = green_occ.shape[0]
    other = [(0, 1), (1, 0)]
    around = [[(i, (i + s) % NZ) for i in range(NZ)] for s in range(NZ)]

    regrouped, *blocks = spread(z.reshape(1), mu_block, tensor)
    arrived = [lax.ppermute(blocks[s], "z", around[s]) if s else blocks[0] for s in range(NZ)]
    q_side = lax.all_to_all(regrouped, ("x", "y"), split_axis=0, concat_axis=0, tiled=True)

    occ = lax.dynamic_index_in_dim(
        green_occ.reshape(orbitals, NZ, NC, -1), core, 2, keepdims=False
    ).reshape(orbitals, -1)
    order = jnp.stack(
        [((z - s) % NZ) * NC + c for s in (1, 2, 3, 0) for c in (core, 1 - core)]
    )
    virt = green_virt.reshape(NZ * NC, -1, orbitals)[order].reshape(orbitals, orbitals).T

    early = make_early(
        mu_block,
        lax.ppermute(mu_block, "core", other),
        blocks[0],
        lax.ppermute(blocks[0], "core", other),
        occ,
    )
    early, virt, last = lax.optimization_barrier((early, virt, arrived[2]))
    arrived = [arrived[1], last, arrived[3]]
    mu_own = listed(mu_block, arrived)
    pieces = [q for p in arrived for q in (p, lax.ppermute(p, "core", other))]
    paired = make_paired(
        z.reshape(1), mu_own, lax.ppermute(mu_own, "core", other), pieces, occ, virt, early
    )
    p_side = lax.all_to_all(
        paired.reshape(NXY * NZ, 3, 32, 256), ("x", "y", "z"), 0, 0, tiled=True
    )
    q_side = q_side.reshape(4, 2, 2, 3, 2, 64, 256)
    given = chi_half((1 - core).reshape(1), p_side, q_side)
    kept = chi_half(core.reshape(1), p_side, q_side)
    chi = (kept + lax.ppermute(given, "core", other)).astype(BF)
    shares = lax.all_to_all(
        chi.reshape(NXY * NZ, 64, 128), ("x", "y", "z"), 0, 0, tiled=True
    )
    return shares.astype(F32).sum(0)


def solution(mesh):
    mesh = Mesh(mesh.devices.reshape(NX, NY, NZ, NC), ("x", "y", "z", "core"))
    return jax.shard_map(
        shards,
        mesh=mesh,
        in_specs=(P(("z", "core"), ("x", "y"), None, None), P(("z", "core"), None), P(), P()),
        out_specs=P(("x", "y"), ("z", "core")),
        check_vma=False,
    )
```

```python
import functools

import jax
import jax.numpy as jnp
from jax import lax
from jax.experimental import pallas as pl
from jax.experimental.pallas import tpu as pltpu
from jax.sharding import Mesh
from jax.sharding import PartitionSpec as P

NX, NY, NZ, NC = 4, 4, 4, 2
NXY = NX * NY
BF, F32 = jnp.bfloat16, jnp.float32
LIMIT = 30 * 1024 * 1024
PAIR_FLOPS = 15_000_000_000


def spread_kernel(mu_ref, tensor_ref, *refs):
    regrouped, blocks = refs[0], refs[1 : 1 + NZ]
    held, turned, listed, mu, in_sems, out_sems, cut_sems, mu_sems = refs[1 + NZ :]
    z_own = lax.axis_index("z")
    count, aux, width, pair = tensor_ref.shape
    part = aux // 2
    loads = [
        pltpu.make_async_copy(
            tensor_ref.at[m, pl.ds(h * part, part)],
            held.at[m, pl.ds(h * part, part)],
            in_sems.at[2 * m + h],
        )
        for m in range(count)
        for h in range(2)
    ]
    for load in loads:
        load.start()
    fetch = pltpu.make_async_copy(mu_ref, mu, mu_sems.at[NZ])
    fetch.start()
    copies = []
    for m in range(count):
        loads[2 * m].wait()
        for h in range(2):
            if h == 1:
                loads[2 * m + 1].wait()
                for s in range(NZ):
                    z = lax.rem(z_own + s, NZ)
                    copies.append(
                        pltpu.make_async_copy(
                            held.at[m, pl.ds(z * 16, 16)],
                            blocks[s].at[m, pl.ds(0, 16)],
                            cut_sems.at[m * NZ + s],
                        )
                    )
                    copies[-1].start()
            rows = held[m, h * part : (h + 1) * part]
            turned[m, h] = jnp.swapaxes(rows, 0, 1).reshape(NXY, 2, part, pair)
            copies.append(
                pltpu.make_async_copy(
                    turned.at[m, h],
                    regrouped.at[:, m, :, pl.ds(h * part, part)],
                    out_sems.at[2 * m + h],
                )
            )
            copies[-1].start()
    fetch.wait()
    lane = lax.broadcasted_iota(jnp.int32, (width, pair), 1)
    for m in range(count):
        tile = jnp.zeros((width, pair), jnp.int32)
        for k in range(mu.shape[1]):
            tile = jnp.where(lane == k, mu[m, k], tile)
        listed[m, 0] = tile.astype(F32).astype(BF)
    for s in range(NZ):
        to = blocks[s].at[:, pl.ds(16, 1)]
        copies.append(pltpu.make_async_copy(listed, to, mu_sems.at[s]))
        copies[-1].start()
    for copy in copies:
        copy.wait()


def spread(mu, tensor):
    blocks, aux, width, pair = tensor.shape
    anywhere = pl.BlockSpec(memory_space=pl.ANY)
    return pl.pallas_call(
        spread_kernel,
        in_specs=[anywhere] * 2,
        out_specs=[anywhere] * (1 + NZ),
        out_shape=[pltpu.HBM((NXY, blocks, 2, aux, pair), BF)]
        + [jax.ShapeDtypeStruct((blocks, 17, width, pair), BF)] * NZ,
        scratch_shapes=[
            pltpu.VMEM(tensor.shape, BF),
            pltpu.VMEM((blocks, 2, NXY, 2, aux // 2, pair), BF),
            pltpu.VMEM((blocks, 1, width, pair), BF),
            pltpu.SMEM(mu.shape, mu.dtype),
            pltpu.SemaphoreType.DMA((2 * blocks,)),
            pltpu.SemaphoreType.DMA((2 * blocks,)),
            pltpu.SemaphoreType.DMA((blocks * NZ,)),
            pltpu.SemaphoreType.DMA((NZ + 1,)),
        ],
        compiler_params=pltpu.CompilerParams(vmem_limit_bytes=60 * 1024 * 1024),
        cost_estimate=pl.CostEstimate(flops=1000, bytes_accessed=1000, transcendentals=0),
    )(mu, tensor)


def gathered(ref, mu, t, per, width):
    return jnp.concatenate(
        [ref[pl.ds(pl.multiple_of(mu[t, k] * width, width), width), :] for k in range(per)],
        axis=0,
    )


def occupied(piece, mu, m, at, occ_ref, stage):
    per, half, width = mu.shape[1], occ_ref.shape[1], 32
    occ = gathered(occ_ref, mu, at[0], per, width)
    got = jnp.dot(
        piece[m, :16].reshape(16 * width, -1), occ, preferred_element_type=F32
    ).astype(BF)
    stage[:, at[1] : at[1] + width, :] = got.reshape(16, width, half)


def early_kernel(mu_own, mu_other, own, other, occ_ref, out_ref, stage):
    stage[:, :64, :] = jnp.zeros((16, 64, stage.shape[2]), BF)
    for n in range(6):
        piece, mu = ((own, mu_own), (other, mu_other))[n // 3]
        occupied(piece, mu, n % 3, (n % 3, 64 + n * 32), occ_ref, stage)
    for p in range(16):
        for g in range(2):
            out_ref[p, :, g * 128 : (g + 1) * 128] = stage[p, g * 128 : (g + 1) * 128].T


def make_early(mu_own, mu_other, own, other, occ):
    half = occ.shape[1]
    vmem = pl.BlockSpec(memory_space=pltpu.VMEM)
    smem = pl.BlockSpec(memory_space=pltpu.SMEM)
    return pl.pallas_call(
        early_kernel,
        in_specs=[smem] * 2 + [vmem] * 3,
        out_specs=vmem,
        out_shape=jax.ShapeDtypeStruct((16, half, 256), BF),
        scratch_shapes=[pltpu.VMEM((16, 256, half), BF)],
        compiler_params=pltpu.CompilerParams(vmem_limit_bytes=LIMIT),
        cost_estimate=pl.CostEstimate(flops=1000, bytes_accessed=1000, transcendentals=0),
    )(mu_own, mu_other, own, other, occ)


def pair_kernel(mu_own, mu_other, *refs):
    pieces, refs = refs[:6], refs[6:]
    occ_ref, virt_ref, early_ref, out_ref, turned, stage, result, out_sems = refs
    per, width, pair = mu_own.shape[1], 32, 256
    z_own = lax.axis_index("z")
    for n in range(18):
        piece, m = divmod(n, 3)
        mu = mu_other if piece % 2 else mu_own
        at = ((piece // 2 + 1) * 3 + m, n % 4 * width)
        occupied(pieces[piece], mu, m, at, occ_ref, stage)
        if n % 4 == 3:
            for p in range(16):
                turned[p, :, (n - 3) * width : (n + 1) * width] = stage[p].T
    turned[:, :, 512:] = early_ref[...]
    for p in range(16):
        turned[p, :, 512:576] = stage[p, :64].T
    stores = []
    for z in range(NZ):
        s = lax.rem(z_own - z + NZ, NZ)
        for m in range(3):
            lam = (z * 3 + m) * width
            left = turned[:, lam : lam + width, :].reshape(16 * width, -1)
            virt = gathered(virt_ref, mu_own, s * 3 + m, per, width)
            got = lax.dot_general(
                left, virt, (((1,), (1,)), ((), ())), preferred_element_type=F32
            ).astype(BF)
            got = jnp.swapaxes(got.reshape(16, width, pair), 0, 1)
            result[z, :, m, :, :] = got.reshape(NXY, 32, pair)
        stores.append(
            pltpu.make_async_copy(result.at[z], out_ref.at[:, z], out_sems.at[z])
        )
        stores[z].start()
    for store in stores:
        store.wait()


def make_paired(mu_own, mu_other, pieces, occ, virt, early):
    orbitals, half = occ.shape
    smem = pl.BlockSpec(memory_space=pltpu.SMEM)
    return pl.pallas_call(
        pair_kernel,
        in_specs=[smem] * 2 + [pl.BlockSpec(memory_space=pltpu.VMEM)] * 9,
        out_specs=pl.BlockSpec(memory_space=pltpu.HBM),
        out_shape=pltpu.HBM((NXY, NZ, 3, 32, 256), BF),
        scratch_shapes=[
            pltpu.VMEM((16, half, orbitals), BF),
            pltpu.VMEM((16, 128, half), BF),
            pltpu.VMEM((NZ, NXY, 3, 32, 256), BF),
            pltpu.SemaphoreType.DMA((NZ,)),
        ],
        compiler_params=pltpu.CompilerParams(vmem_limit_bytes=LIMIT),
        cost_estimate=pl.CostEstimate(
            flops=PAIR_FLOPS, bytes_accessed=12_000_000, transcendentals=0
        ),
    )(mu_own, mu_other, *pieces, occ, virt, early)


def listed_kernel(mu_ref, *refs):
    per = mu_ref.shape[1]
    refs[-1][:3] = mu_ref[...]
    for s in range(1, NZ):
        refs[-1][s * 3 : s * 3 + 3] = refs[s - 1][:, 0, 0, :per].astype(F32).astype(jnp.int32)


def listed(mu_block, pieces):
    blocks, per = mu_block.shape
    tile = pl.BlockSpec((blocks, 1, 32, 256), lambda i: (0, 16, 0, 0))
    return pl.pallas_call(
        listed_kernel,
        grid=(1,),
        in_specs=[pl.BlockSpec((blocks, per), lambda i: (0, 0))] + [tile] * 3,
        out_specs=pl.BlockSpec((NZ * blocks, per), lambda i: (0, 0)),
        out_shape=jax.ShapeDtypeStruct((NZ * blocks, per), jnp.int32),
        compiler_params=pltpu.CompilerParams(vmem_limit_bytes=LIMIT),
    )(mu_block, *pieces)


def chi_kernel(far, a_ref, b_ref, out_ref, held, total, sems):
    pair = a_ref.shape[-1]
    core = lax.rem(lax.axis_index("core") + far, NC)
    loads = [
        pltpu.make_async_copy(b_ref.at[:, core, :, m], held.at[m], sems.at[m])
        for m in range(3)
    ]
    for load in loads:
        load.start()
    for m in range(3):
        loads[m].wait()
        b = jnp.concatenate([held[m, :, :, r].reshape(-1, pair) for r in range(2)], axis=1)
        for i in range(2):
            a = jnp.concatenate(
                [
                    a_ref[i * 32 : (i + 1) * 32, m, r * 16 : (r + 1) * 16, :].reshape(-1, pair)
                    for r in range(2)
                ],
                axis=1,
            )
            got = lax.dot_general(a, b, (((1,), (1,)), ((), ())), preferred_element_type=F32)
            if m == 0:
                total[i] = got
            elif m == 1:
                total[i] += got
            else:
                got += total[i]
                for z in range(NZ):
                    out_ref[i * 8 : (i + 1) * 8, z] = got[:, z * 128 : (z + 1) * 128].reshape(
                        -1, 64, 128
                    )


def chi_half(far, a, b):
    vmem = pl.BlockSpec(memory_space=pltpu.VMEM)
    return pl.pallas_call(
        functools.partial(chi_kernel, far),
        in_specs=[
            vmem,
            pl.BlockSpec(memory_space=pl.ANY),
        ],
        out_specs=vmem,
        out_shape=jax.ShapeDtypeStruct((NXY, NZ, 64, 128), F32),
        scratch_shapes=[
            pltpu.VMEM((3, 4, 2, 2, 64, 256), BF),
            pltpu.VMEM((2, 512, 512), F32),
            pltpu.SemaphoreType.DMA((3,)),
        ],
        compiler_params=pltpu.CompilerParams(vmem_limit_bytes=LIMIT),
        cost_estimate=pl.CostEstimate(
            flops=1_700_000_000, bytes_accessed=7_000_000, transcendentals=0
        ),
    )(a, b)


def shards(tensor, mu_block, green_occ, green_virt):
    z, core = lax.axis_index("z"), lax.axis_index("core")
    orbitals = green_occ.shape[0]
    other = [(0, 1), (1, 0)]
    around = [[(i, (i + s) % NZ) for i in range(NZ)] for s in range(NZ)]

    regrouped, *blocks = spread(mu_block, tensor)
    arrived = [lax.ppermute(blocks[s], "z", around[s]) if s else blocks[0] for s in range(NZ)]
    q_side = lax.all_to_all(regrouped, ("x", "y"), split_axis=0, concat_axis=0, tiled=True)

    occ = lax.dynamic_index_in_dim(
        green_occ.reshape(orbitals, NZ, NC, -1), core, 2, keepdims=False
    ).reshape(orbitals, -1)
    order = jnp.stack(
        [((z - s) % NZ) * NC + c for s in (1, 2, 3, 0) for c in (core, 1 - core)]
    )
    virt = green_virt.reshape(NZ * NC, -1, orbitals)[order].reshape(orbitals, orbitals).T

    early = make_early(
        mu_block,
        lax.ppermute(mu_block, "core", other),
        blocks[0],
        lax.ppermute(blocks[0], "core", other),
        occ,
    )
    early, virt, last = lax.optimization_barrier((early, virt, arrived[2]))
    arrived = [arrived[1], last, arrived[3]]
    mu_own = listed(mu_block, arrived)
    pieces = [q for p in arrived for q in (p, lax.ppermute(p, "core", other))]
    paired = make_paired(
        mu_own, lax.ppermute(mu_own, "core", other), pieces, occ, virt, early
    )
    p_side = lax.all_to_all(
        paired.reshape(NXY * NZ, 3, 32, 256), ("x", "y", "z"), 0, 0, tiled=True
    )
    q_side = q_side.reshape(4, 2, 2, 3, 2, 64, 256)
    given = chi_half(1, p_side, q_side)
    kept = chi_half(0, p_side, q_side)
    chi = (kept + lax.ppermute(given, "core", other)).astype(BF)
    shares = lax.all_to_all(
        chi.reshape(NXY * NZ, 64, 128), ("x", "y", "z"), 0, 0, tiled=True
    )
    return shares.astype(F32).sum(0)


def solution(mesh):
    mesh = Mesh(mesh.devices.reshape(NX, NY, NZ, NC), ("x", "y", "z", "core"))
    return jax.shard_map(
        shards,
        mesh=mesh,
        in_specs=(P(("z", "core"), ("x", "y"), None, None), P(("z", "core"), None), P(), P()),
        out_specs=P(("x", "y"), ("z", "core")),
        check_vma=False,
    )
```

```python
import functools

import jax
import jax.numpy as jnp
from jax import lax
from jax.experimental import pallas as pl
from jax.experimental.pallas import tpu as pltpu
from jax.sharding import Mesh
from jax.sharding import PartitionSpec as P

NX, NY, NZ, NC = 4, 4, 4, 2
NXY = NX * NY
BF, F32 = jnp.bfloat16, jnp.float32
LIMIT = 30 * 1024 * 1024
PAIR_FLOPS = 15_000_000_000


def spread_kernel(mu_ref, tensor_ref, *refs):
    regrouped, blocks = refs[0], refs[1 : 1 + NZ]
    held, turned, listed, mu, in_sems, out_sems, cut_sems, mu_sems = refs[1 + NZ :]
    z_own = lax.axis_index("z")
    count, aux, width, pair = tensor_ref.shape
    part = aux // 2
    loads = [
        pltpu.make_async_copy(
            tensor_ref.at[m, pl.ds(h * part, part)],
            held.at[m, pl.ds(h * part, part)],
            in_sems.at[2 * m + h],
        )
        for m in range(count)
        for h in range(2)
    ]
    for load in loads:
        load.start()
    fetch = pltpu.make_async_copy(mu_ref, mu, mu_sems.at[NZ])
    fetch.start()
    copies = []
    for m in range(count):
        loads[2 * m].wait()
        for h in range(2):
            if h == 1:
                loads[2 * m + 1].wait()
                for s in range(NZ):
                    z = lax.rem(z_own + s, NZ)
                    copies.append(
                        pltpu.make_async_copy(
                            held.at[m, pl.ds(z * 16, 16)],
                            blocks[s].at[m, pl.ds(0, 16)],
                            cut_sems.at[m * NZ + s],
                        )
                    )
                    copies[-1].start()
            rows = held[m, h * part : (h + 1) * part]
            turned[m, h] = jnp.swapaxes(rows, 0, 1).reshape(NXY, 2, part, pair)
            copies.append(
                pltpu.make_async_copy(
                    turned.at[m, h],
                    regrouped.at[:, m, :, pl.ds(h * part, part)],
                    out_sems.at[2 * m + h],
                )
            )
            copies[-1].start()
    fetch.wait()
    lane = lax.broadcasted_iota(jnp.int32, (width, pair), 1)
    for m in range(count):
        tile = jnp.zeros((width, pair), jnp.int32)
        for k in range(mu.shape[1]):
            tile = jnp.where(lane == k, mu[m, k], tile)
        listed[m, 0] = tile.astype(F32).astype(BF)
    for s in range(NZ):
        to = blocks[s].at[:, pl.ds(16, 1)]
        copies.append(pltpu.make_async_copy(listed, to, mu_sems.at[s]))
        copies[-1].start()
    for copy in copies:
        copy.wait()


def spread(mu, tensor):
    blocks, aux, width, pair = tensor.shape
    anywhere = pl.BlockSpec(memory_space=pl.ANY)
    return pl.pallas_call(
        spread_kernel,
        in_specs=[anywhere] * 2,
        out_specs=[anywhere] * (1 + NZ),
        out_shape=[pltpu.HBM((NXY, blocks, 2, aux, pair), BF)]
        + [jax.ShapeDtypeStruct((blocks, 17, width, pair), BF)] * NZ,
        scratch_shapes=[
            pltpu.VMEM(tensor.shape, BF),
            pltpu.VMEM((blocks, 2, NXY, 2, aux // 2, pair), BF),
            pltpu.VMEM((blocks, 1, width, pair), BF),
            pltpu.SMEM(mu.shape, mu.dtype),
            pltpu.SemaphoreType.DMA((2 * blocks,)),
            pltpu.SemaphoreType.DMA((2 * blocks,)),
            pltpu.SemaphoreType.DMA((blocks * NZ,)),
            pltpu.SemaphoreType.DMA((NZ + 1,)),
        ],
        compiler_params=pltpu.CompilerParams(vmem_limit_bytes=60 * 1024 * 1024),
        cost_estimate=pl.CostEstimate(flops=1000, bytes_accessed=1000, transcendentals=0),
    )(mu, tensor)


def gathered(ref, mu, t, per, width):
    return jnp.concatenate(
        [ref[pl.ds(pl.multiple_of(mu[t, k] * width, width), width), :] for k in range(per)],
        axis=0,
    )


def occupied(piece, mu, m, at, occ_ref, stage):
    per, half, width = mu.shape[1], occ_ref.shape[1], 32
    occ = gathered(occ_ref, mu, at[0], per, width)
    got = jnp.dot(
        piece[m, :16].reshape(16 * width, -1), occ, preferred_element_type=F32
    ).astype(BF)
    stage[:, at[1] : at[1] + width, :] = got.reshape(16, width, half)


def early_kernel(mu_own, mu_other, own, other, occ_ref, out_ref, stage):
    stage[:, :64, :] = jnp.zeros((16, 64, stage.shape[2]), BF)
    for n in range(6):
        piece, mu = ((own, mu_own), (other, mu_other))[n // 3]
        occupied(piece, mu, n % 3, (n % 3, 64 + n * 32), occ_ref, stage)
    for p in range(16):
        for g in range(2):
            out_ref[p, :, g * 128 : (g + 1) * 128] = stage[p, g * 128 : (g + 1) * 128].T


def make_early(mu_own, mu_other, own, other, occ):
    half = occ.shape[1]
    vmem = pl.BlockSpec(memory_space=pltpu.VMEM)
    smem = pl.BlockSpec(memory_space=pltpu.SMEM)
    return pl.pallas_call(
        early_kernel,
        in_specs=[smem] * 2 + [vmem] * 3,
        out_specs=vmem,
        out_shape=jax.ShapeDtypeStruct((16, half, 256), BF),
        scratch_shapes=[pltpu.VMEM((16, 256, half), BF)],
        compiler_params=pltpu.CompilerParams(vmem_limit_bytes=LIMIT),
        cost_estimate=pl.CostEstimate(flops=1000, bytes_accessed=1000, transcendentals=0),
    )(mu_own, mu_other, own, other, occ)


def pair_kernel(mu_own, mu_other, *refs):
    pieces, refs = refs[:6], refs[6:]
    occ_ref, virt_ref, early_ref, out_ref, turned, stage, result, out_sems = refs
    per, width, pair = mu_own.shape[1], 32, 256
    z_own = lax.axis_index("z")
    for n in range(18):
        piece, m = divmod(n, 3)
        mu = mu_other if piece % 2 else mu_own
        at = ((piece // 2 + 1) * 3 + m, n % 4 * width)
        occupied(pieces[piece], mu, m, at, occ_ref, stage)
        if n % 4 == 3:
            for p in range(16):
                turned[p, :, (n - 3) * width : (n + 1) * width] = stage[p].T
    turned[:, :, 512:] = early_ref[...]
    for p in range(16):
        turned[p, :, 512:576] = stage[p, :64].T
    stores = []
    for z in range(NZ):
        s = lax.rem(z_own - z + NZ, NZ)
        for m in range(3):
            lam = (z * 3 + m) * width
            left = turned[:, lam : lam + width, :].reshape(16 * width, -1)
            virt = gathered(virt_ref, mu_own, s * 3 + m, per, width)
            got = lax.dot_general(
                left, virt, (((1,), (1,)), ((), ())), preferred_element_type=F32
            ).astype(BF)
            got = jnp.swapaxes(got.reshape(16, width, pair), 0, 1)
            result[z, :, m, :, :] = got.reshape(NXY, 32, pair)
        stores.append(
            pltpu.make_async_copy(result.at[z], out_ref.at[:, z], out_sems.at[z])
        )
        stores[z].start()
    for store in stores:
        store.wait()


def make_paired(mu_own, mu_other, pieces, occ, virt, early):
    orbitals, half = occ.shape
    smem = pl.BlockSpec(memory_space=pltpu.SMEM)
    return pl.pallas_call(
        pair_kernel,
        in_specs=[smem] * 2 + [pl.BlockSpec(memory_space=pltpu.VMEM)] * 9,
        out_specs=pl.BlockSpec(memory_space=pltpu.HBM),
        out_shape=pltpu.HBM((NXY, NZ, 3, 32, 256), BF),
        scratch_shapes=[
            pltpu.VMEM((16, half, orbitals), BF),
            pltpu.VMEM((16, 128, half), BF),
            pltpu.VMEM((NZ, NXY, 3, 32, 256), BF),
            pltpu.SemaphoreType.DMA((NZ,)),
        ],
        compiler_params=pltpu.CompilerParams(vmem_limit_bytes=LIMIT),
        cost_estimate=pl.CostEstimate(
            flops=PAIR_FLOPS, bytes_accessed=12_000_000, transcendentals=0
        ),
    )(mu_own, mu_other, *pieces, occ, virt, early)


def listed_kernel(mu_ref, *refs):
    per = mu_ref.shape[1]
    refs[-1][:3] = mu_ref[...]
    for s in range(1, NZ):
        refs[-1][s * 3 : s * 3 + 3] = refs[s - 1][:, 0, 0, :per].astype(F32).astype(jnp.int32)


def listed(mu_block, pieces):
    blocks, per = mu_block.shape
    tile = pl.BlockSpec((blocks, 1, 32, 256), lambda i: (0, 16, 0, 0))
    return pl.pallas_call(
        listed_kernel,
        grid=(1,),
        in_specs=[pl.BlockSpec((blocks, per), lambda i: (0, 0))] + [tile] * 3,
        out_specs=pl.BlockSpec((NZ * blocks, per), lambda i: (0, 0)),
        out_shape=jax.ShapeDtypeStruct((NZ * blocks, per), jnp.int32),
        compiler_params=pltpu.CompilerParams(vmem_limit_bytes=LIMIT),
    )(mu_block, *pieces)


def chi_kernel(far, a_ref, b_ref, out_ref, held, total, sems):
    pair = a_ref.shape[-1]
    core = lax.rem(lax.axis_index("core") + far, NC)
    loads = [
        pltpu.make_async_copy(b_ref.at[:, core, :, m], held.at[m], sems.at[m])
        for m in range(3)
    ]
    for load in loads:
        load.start()
    for m in range(3):
        loads[m].wait()
        b = jnp.concatenate([held[m, :, :, r].reshape(-1, pair) for r in range(2)], axis=1)
        for i in range(2):
            a = jnp.concatenate(
                [
                    a_ref[i * 32 : (i + 1) * 32, m, r * 16 : (r + 1) * 16, :].reshape(-1, pair)
                    for r in range(2)
                ],
                axis=1,
            )
            got = lax.dot_general(a, b, (((1,), (1,)), ((), ())), preferred_element_type=F32)
            if m == 0:
                total[i] = got
            elif m == 1:
                total[i] += got
            else:
                got += total[i]
                for z in range(NZ):
                    out_ref[i * 8 : (i + 1) * 8, z] = got[:, z * 128 : (z + 1) * 128].reshape(
                        -1, 64, 128
                    ).astype(out_ref.dtype)


def chi_half(far, a, b, kind):
    vmem = pl.BlockSpec(memory_space=pltpu.VMEM)
    return pl.pallas_call(
        functools.partial(chi_kernel, far),
        in_specs=[
            vmem,
            pl.BlockSpec(memory_space=pl.ANY),
        ],
        out_specs=vmem,
        out_shape=jax.ShapeDtypeStruct((NXY, NZ, 64, 128), kind),
        scratch_shapes=[
            pltpu.VMEM((3, 4, 2, 2, 64, 256), BF),
            pltpu.VMEM((2, 512, 512), F32),
            pltpu.SemaphoreType.DMA((3,)),
        ],
        compiler_params=pltpu.CompilerParams(vmem_limit_bytes=LIMIT),
        cost_estimate=pl.CostEstimate(
            flops=1_700_000_000, bytes_accessed=7_000_000, transcendentals=0
        ),
    )(a, b)


def shards(tensor, mu_block, green_occ, green_virt):
    z, core = lax.axis_index("z"), lax.axis_index("core")
    orbitals = green_occ.shape[0]
    other = [(0, 1), (1, 0)]
    around = [[(i, (i + s) % NZ) for i in range(NZ)] for s in range(NZ)]

    regrouped, *blocks = spread(mu_block, tensor)
    arrived = [lax.ppermute(blocks[s], "z", around[s]) if s else blocks[0] for s in range(NZ)]
    q_side = lax.all_to_all(regrouped, ("x", "y"), split_axis=0, concat_axis=0, tiled=True)

    occ = lax.dynamic_index_in_dim(
        green_occ.reshape(orbitals, NZ, NC, -1), core, 2, keepdims=False
    ).reshape(orbitals, -1)
    order = jnp.stack(
        [((z - s) % NZ) * NC + c for s in (1, 2, 3, 0) for c in (core, 1 - core)]
    )
    virt = green_virt.reshape(NZ * NC, -1, orbitals)[order].reshape(orbitals, orbitals).T

    early = make_early(
        mu_block,
        lax.ppermute(mu_block, "core", other),
        blocks[0],
        lax.ppermute(blocks[0], "core", other),
        occ,
    )
    early, virt, last = lax.optimization_barrier((early, virt, arrived[2]))
    arrived = [arrived[1], last, arrived[3]]
    mu_own = listed(mu_block, arrived)
    pieces = [q for p in arrived for q in (p, lax.ppermute(p, "core", other))]
    paired = make_paired(
        mu_own, lax.ppermute(mu_own, "core", other), pieces, occ, virt, early
    )
    p_side = lax.all_to_all(
        paired.reshape(NXY * NZ, 3, 32, 256), ("x", "y", "z"), 0, 0, tiled=True
    )
    q_side = q_side.reshape(4, 2, 2, 3, 2, 64, 256)
    given = chi_half(1, p_side, q_side, BF)
    kept = chi_half(0, p_side, q_side, F32)
    chi = (kept + lax.ppermute(given, "core", other)).astype(BF)
    shares = lax.all_to_all(
        chi.reshape(NXY * NZ, 64, 128), ("x", "y", "z"), 0, 0, tiled=True
    )
    return shares.astype(F32).sum(0)


def solution(mesh):
    mesh = Mesh(mesh.devices.reshape(NX, NY, NZ, NC), ("x", "y", "z", "core"))
    return jax.shard_map(
        shards,
        mesh=mesh,
        in_specs=(P(("z", "core"), ("x", "y"), None, None), P(("z", "core"), None), P(), P()),
        out_specs=P(("x", "y"), ("z", "core")),
        check_vma=False,
    )
```

```python
import functools

import jax
import jax.numpy as jnp
from jax import lax
from jax.experimental import pallas as pl
from jax.experimental.pallas import tpu as pltpu
from jax.sharding import Mesh
from jax.sharding import PartitionSpec as P

NX, NY, NZ, NC = 4, 4, 4, 2
NXY = NX * NY
BF, F32 = jnp.bfloat16, jnp.float32
LIMIT = 30 * 1024 * 1024
PAIR_FLOPS = 15_000_000_000


def spread_kernel(mu_ref, tensor_ref, *refs):
    regrouped, blocks = refs[0], refs[1 : 1 + NZ]
    held, turned, listed, mu, in_sems, out_sems, cut_sems, mu_sems = refs[1 + NZ :]
    z_own = lax.axis_index("z")
    count, aux, width, pair = tensor_ref.shape
    part = aux // 2
    loads = [
        pltpu.make_async_copy(
            tensor_ref.at[m, pl.ds(h * part, part)],
            held.at[m, pl.ds(h * part, part)],
            in_sems.at[2 * m + h],
        )
        for m in range(count)
        for h in range(2)
    ]
    for load in loads:
        load.start()
    fetch = pltpu.make_async_copy(mu_ref, mu, mu_sems.at[NZ])
    fetch.start()
    copies = []
    for m in range(count):
        loads[2 * m].wait()
        for h in range(2):
            if h == 1:
                loads[2 * m + 1].wait()
                for s in range(NZ):
                    z = lax.rem(z_own + s, NZ)
                    copies.append(
                        pltpu.make_async_copy(
                            held.at[m, pl.ds(z * 16, 16)],
                            blocks[s].at[m, pl.ds(0, 16)],
                            cut_sems.at[m * NZ + s],
                        )
                    )
                    copies[-1].start()
            rows = held[m, h * part : (h + 1) * part]
            turned[m, h] = jnp.swapaxes(rows, 0, 1).reshape(NXY, 2, part, pair)
            copies.append(
                pltpu.make_async_copy(
                    turned.at[m, h],
                    regrouped.at[:, m, :, pl.ds(h * part, part)],
                    out_sems.at[2 * m + h],
                )
            )
            copies[-1].start()
    fetch.wait()
    lane = lax.broadcasted_iota(jnp.int32, (width, pair), 1)
    for m in range(count):
        tile = jnp.zeros((width, pair), jnp.int32)
        for k in range(mu.shape[1]):
            tile = jnp.where(lane == k, mu[m, k], tile)
        listed[m, 0] = tile.astype(F32).astype(BF)
    for s in range(NZ):
        to = blocks[s].at[:, pl.ds(16, 1)]
        copies.append(pltpu.make_async_copy(listed, to, mu_sems.at[s]))
        copies[-1].start()
    for copy in copies:
        copy.wait()


def spread(mu, tensor):
    blocks, aux, width, pair = tensor.shape
    anywhere = pl.BlockSpec(memory_space=pl.ANY)
    return pl.pallas_call(
        spread_kernel,
        in_specs=[anywhere] * 2,
        out_specs=[anywhere] * (1 + NZ),
        out_shape=[pltpu.HBM((NXY, blocks, 2, aux, pair), BF)]
        + [jax.ShapeDtypeStruct((blocks, 17, width, pair), BF)] * NZ,
        scratch_shapes=[
            pltpu.VMEM(tensor.shape, BF),
            pltpu.VMEM((blocks, 2, NXY, 2, aux // 2, pair), BF),
            pltpu.VMEM((blocks, 1, width, pair), BF),
            pltpu.SMEM(mu.shape, mu.dtype),
            pltpu.SemaphoreType.DMA((2 * blocks,)),
            pltpu.SemaphoreType.DMA((2 * blocks,)),
            pltpu.SemaphoreType.DMA((blocks * NZ,)),
            pltpu.SemaphoreType.DMA((NZ + 1,)),
        ],
        compiler_params=pltpu.CompilerParams(vmem_limit_bytes=60 * 1024 * 1024),
        cost_estimate=pl.CostEstimate(flops=1000, bytes_accessed=1000, transcendentals=0),
    )(mu, tensor)


def gathered(ref, mu, t, per, width):
    return jnp.concatenate(
        [ref[pl.ds(pl.multiple_of(mu[t, k] * width, width), width), :] for k in range(per)],
        axis=0,
    )


def occupied(piece, mu, m, at, occ_ref, stage):
    per, half, width = mu.shape[1], occ_ref.shape[1], 32
    occ = gathered(occ_ref, mu, at[0], per, width)
    got = jnp.dot(
        piece[m, :16].reshape(16 * width, -1), occ, preferred_element_type=F32
    ).astype(BF)
    stage[:, at[1] : at[1] + width, :] = got.reshape(16, width, half)


def early_kernel(mu_own, mu_other, own, other, occ_ref, out_ref, stage):
    stage[:, :64, :] = jnp.zeros((16, 64, stage.shape[2]), BF)
    for n in range(6):
        piece, mu = ((own, mu_own), (other, mu_other))[n // 3]
        occupied(piece, mu, n % 3, (n % 3, 64 + n * 32), occ_ref, stage)
    for p in range(16):
        for g in range(2):
            out_ref[p, :, g * 128 : (g + 1) * 128] = stage[p, g * 128 : (g + 1) * 128].T


def make_early(mu_own, mu_other, own, other, occ):
    half = occ.shape[1]
    vmem = pl.BlockSpec(memory_space=pltpu.VMEM)
    smem = pl.BlockSpec(memory_space=pltpu.SMEM)
    return pl.pallas_call(
        early_kernel,
        in_specs=[smem] * 2 + [vmem] * 3,
        out_specs=vmem,
        out_shape=jax.ShapeDtypeStruct((16, half, 256), BF),
        scratch_shapes=[pltpu.VMEM((16, 256, half), BF)],
        compiler_params=pltpu.CompilerParams(vmem_limit_bytes=LIMIT),
        cost_estimate=pl.CostEstimate(flops=1000, bytes_accessed=1000, transcendentals=0),
    )(mu_own, mu_other, own, other, occ)


def pair_kernel(mu_own, mu_other, *refs):
    pieces, refs = refs[:6], refs[6:]
    occ_ref, virt_ref, early_ref, out_ref, turned, stage, result, out_sems, early_sem = refs
    early = pltpu.make_async_copy(early_ref, turned.at[:, :, 512:], early_sem)
    early.start()
    per, width, pair = mu_own.shape[1], 32, 256
    z_own = lax.axis_index("z")
    for n in range(18):
        piece, m = divmod(n, 3)
        mu = mu_other if piece % 2 else mu_own
        at = ((piece // 2 + 1) * 3 + m, n % 4 * width)
        occupied(pieces[piece], mu, m, at, occ_ref, stage)
        if n % 4 == 3:
            for p in range(16):
                turned[p, :, (n - 3) * width : (n + 1) * width] = stage[p].T
    early.wait()
    for p in range(16):
        turned[p, :, 512:576] = stage[p, :64].T
    stores = []
    for z in range(NZ):
        s = lax.rem(z_own - z + NZ, NZ)
        for m in range(3):
            lam = (z * 3 + m) * width
            left = turned[:, lam : lam + width, :].reshape(16 * width, -1)
            virt = gathered(virt_ref, mu_own, s * 3 + m, per, width)
            got = lax.dot_general(
                left, virt, (((1,), (1,)), ((), ())), preferred_element_type=F32
            ).astype(BF)
            got = jnp.swapaxes(got.reshape(16, width, pair), 0, 1)
            result[z, :, m, :, :] = got.reshape(NXY, 32, pair)
        stores.append(
            pltpu.make_async_copy(result.at[z], out_ref.at[:, z], out_sems.at[z])
        )
        stores[z].start()
    for store in stores:
        store.wait()


def make_paired(mu_own, mu_other, pieces, occ, virt, early):
    orbitals, half = occ.shape
    smem = pl.BlockSpec(memory_space=pltpu.SMEM)
    return pl.pallas_call(
        pair_kernel,
        in_specs=[smem] * 2 + [pl.BlockSpec(memory_space=pltpu.VMEM)] * 9,
        out_specs=pl.BlockSpec(memory_space=pltpu.HBM),
        out_shape=pltpu.HBM((NXY, NZ, 3, 32, 256), BF),
        scratch_shapes=[
            pltpu.VMEM((16, half, orbitals), BF),
            pltpu.VMEM((16, 128, half), BF),
            pltpu.VMEM((NZ, NXY, 3, 32, 256), BF),
            pltpu.SemaphoreType.DMA((NZ,)),
            pltpu.SemaphoreType.DMA,
        ],
        compiler_params=pltpu.CompilerParams(vmem_limit_bytes=LIMIT),
        cost_estimate=pl.CostEstimate(
            flops=PAIR_FLOPS, bytes_accessed=12_000_000, transcendentals=0
        ),
    )(mu_own, mu_other, *pieces, occ, virt, early)


def listed_kernel(mu_ref, *refs):
    per = mu_ref.shape[1]
    refs[-1][:3] = mu_ref[...]
    for s in range(1, NZ):
        refs[-1][s * 3 : s * 3 + 3] = refs[s - 1][:, 0, 0, :per].astype(F32).astype(jnp.int32)


def listed(mu_block, pieces):
    blocks, per = mu_block.shape
    tile = pl.BlockSpec((blocks, 1, 32, 256), lambda i: (0, 16, 0, 0))
    return pl.pallas_call(
        listed_kernel,
        grid=(1,),
        in_specs=[pl.BlockSpec((blocks, per), lambda i: (0, 0))] + [tile] * 3,
        out_specs=pl.BlockSpec((NZ * blocks, per), lambda i: (0, 0)),
        out_shape=jax.ShapeDtypeStruct((NZ * blocks, per), jnp.int32),
        compiler_params=pltpu.CompilerParams(vmem_limit_bytes=LIMIT),
    )(mu_block, *pieces)


def chi_kernel(far, a_ref, b_ref, out_ref, held, total, sems):
    pair = a_ref.shape[-1]
    core = lax.rem(lax.axis_index("core") + far, NC)
    loads = [
        pltpu.make_async_copy(b_ref.at[:, core, :, m], held.at[m], sems.at[m])
        for m in range(3)
    ]
    for load in loads:
        load.start()
    for m in range(3):
        loads[m].wait()
        b = jnp.concatenate([held[m, :, :, r].reshape(-1, pair) for r in range(2)], axis=1)
        for i in range(2):
            a = jnp.concatenate(
                [
                    a_ref[i * 32 : (i + 1) * 32, m, r * 16 : (r + 1) * 16, :].reshape(-1, pair)
                    for r in range(2)
                ],
                axis=1,
            )
            got = lax.dot_general(a, b, (((1,), (1,)), ((), ())), preferred_element_type=F32)
            if m == 0:
                total[i] = got
            elif m == 1:
                total[i] += got
            else:
                got += total[i]
                for z in range(NZ):
                    out_ref[i * 8 : (i + 1) * 8, z] = got[:, z * 128 : (z + 1) * 128].reshape(
                        -1, 64, 128
                    ).astype(out_ref.dtype)


def chi_half(far, a, b, kind):
    vmem = pl.BlockSpec(memory_space=pltpu.VMEM)
    return pl.pallas_call(
        functools.partial(chi_kernel, far),
        in_specs=[
            vmem,
            pl.BlockSpec(memory_space=pl.ANY),
        ],
        out_specs=vmem,
        out_shape=jax.ShapeDtypeStruct((NXY, NZ, 64, 128), kind),
        scratch_shapes=[
            pltpu.VMEM((3, 4, 2, 2, 64, 256), BF),
            pltpu.VMEM((2, 512, 512), F32),
            pltpu.SemaphoreType.DMA((3,)),
        ],
        compiler_params=pltpu.CompilerParams(vmem_limit_bytes=LIMIT),
        cost_estimate=pl.CostEstimate(
            flops=1_700_000_000, bytes_accessed=7_000_000, transcendentals=0
        ),
    )(a, b)


def shards(tensor, mu_block, green_occ, green_virt):
    z, core = lax.axis_index("z"), lax.axis_index("core")
    orbitals = green_occ.shape[0]
    other = [(0, 1), (1, 0)]
    around = [[(i, (i + s) % NZ) for i in range(NZ)] for s in range(NZ)]

    regrouped, *blocks = spread(mu_block, tensor)
    arrived = [lax.ppermute(blocks[s], "z", around[s]) if s else blocks[0] for s in range(NZ)]
    q_side = lax.all_to_all(regrouped, ("x", "y"), split_axis=0, concat_axis=0, tiled=True)

    occ = lax.dynamic_index_in_dim(
        green_occ.reshape(orbitals, NZ, NC, -1), core, 2, keepdims=False
    ).reshape(orbitals, -1)
    order = jnp.stack(
        [((z - s) % NZ) * NC + c for s in (1, 2, 3, 0) for c in (core, 1 - core)]
    )
    virt = green_virt.reshape(NZ * NC, -1, orbitals)[order].reshape(orbitals, orbitals).T

    early = make_early(
        mu_block,
        lax.ppermute(mu_block, "core", other),
        blocks[0],
        lax.ppermute(blocks[0], "core", other),
        occ,
    )
    early, virt, last = lax.optimization_barrier((early, virt, arrived[2]))
    arrived = [arrived[1], last, arrived[3]]
    mu_own = listed(mu_block, arrived)
    pieces = [q for p in arrived for q in (p, lax.ppermute(p, "core", other))]
    paired = make_paired(
        mu_own, lax.ppermute(mu_own, "core", other), pieces, occ, virt, early
    )
    p_side = lax.all_to_all(
        paired.reshape(NXY * NZ, 3, 32, 256), ("x", "y", "z"), 0, 0, tiled=True
    )
    q_side = q_side.reshape(4, 2, 2, 3, 2, 64, 256)
    given = chi_half(1, p_side, q_side, BF)
    kept = chi_half(0, p_side, q_side, F32)
    chi = (kept + lax.ppermute(given, "core", other)).astype(BF)
    shares = lax.all_to_all(
        chi.reshape(NXY * NZ, 64, 128), ("x", "y", "z"), 0, 0, tiled=True
    )
    return shares.astype(F32).sum(0)


def solution(mesh):
    mesh = Mesh(mesh.devices.reshape(NX, NY, NZ, NC), ("x", "y", "z", "core"))
    return jax.shard_map(
        shards,
        mesh=mesh,
        in_specs=(P(("z", "core"), ("x", "y"), None, None), P(("z", "core"), None), P(), P()),
        out_specs=P(("x", "y"), ("z", "core")),
        check_vma=False,
    )
```
